32 devices in a mesh: sub: 8 (over z, x), col: 4 (over y, core).
Axes of the slice: x: 2, y: 2, z: 4, core: 2. Of those that a mesh axis runs over, the one named last changes fastest.
Arguments:
- control: float32 [768, 1536, 32], P('sub', 'col'), may hold values from -6 to 6
- scale_index: int32 [32], replicated, may hold values from 0 to 7
- length_x: float32 [8, 3], replicated, may hold values from 3 to 150
- length_y: float32 [8, 3], replicated, may hold values from 3 to 80
- scale_weight: float32 [8, 3], replicated, may hold values from 0.3 to 1
Outputs:
- increment: float32 [768, 1536, 32], P('sub', 'col')
- wind: bfloat16 [2, 768, 1536, 32], P(None, 'sub', 'col')
The draws below stay inside these ranges and needn't reach their ends.
All inputs are finite; a program needn't handle non-finite values.
Results may differ from the reference program's by a relative error of at most 0.001.
Values sent between devices are 32-bit elements; how exact they have to be, the bound alone decides.
A program may use at most 128 MiB of HBM per device.

```python
import math
import jax
import jax.numpy as jnp
from jax import lax

NX = 1536
NY = 768
SCALES = 3
KINDS = 8
SLABS = 32


def set_ends(result, key, smallest, largest):
    shape = result.shape
    spot = [jax.random.randint(jax.random.fold_in(key, axis), (), 0, shape[axis]) for axis in range(len(shape))]
    result = result.at[tuple(spot)].set(smallest)
    longest = shape.index(max(shape))
    spot[longest] = (spot[longest] + 1) % shape[longest]
    return result.at[tuple(spot)].set(largest)


def steps_of(rng, extent, cuts, smallest, top_value):
    factor_of, own = 1.0, jax.random.fold_in(rng, 6)
    for axis_at, parts in cuts:
        draws = jnp.exp(jax.random.uniform(jax.random.fold_in(own, axis_at), (parts,), jnp.float32, smallest / len(cuts), top_value / len(cuts)))
        factor_of = factor_of * jnp.repeat(draws, extent[axis_at] // parts).reshape([-1 if axis == axis_at else 1 for axis in range(len(extent))])
    return factor_of


def centred(stream_key, extent, scale, reach, cuts=(), dtype=jnp.bfloat16):
    level = steps_of(stream_key, extent, cuts, -0.22, 0.18) if cuts else 1.0
    values = jax.random.normal(stream_key, extent, jnp.float32) * scale * level
    return jnp.minimum(jnp.maximum(values, -reach), reach).astype(dtype)


def setup_inputs(seed: int = 0) -> dict:
    arg_keys = jax.random.split(jax.random.key(seed), 6)
    control = centred(arg_keys[0], (NY, NX, SLABS), 1.0, 6.0, ((0, 8), (1, 4)), jnp.float32)
    scale_index = set_ends(jax.random.randint(arg_keys[1], (SLABS,), 0, KINDS), jax.random.fold_in(arg_keys[1], 1), 0, KINDS - 1).astype(jnp.int32)
    length_x = jnp.clip(jnp.exp(jax.random.uniform(arg_keys[2], (KINDS, SCALES), jnp.float32, math.log(3.0), math.log(150.0))), 3.0, 150.0)
    length_y = jnp.clip(jnp.exp(jax.random.uniform(arg_keys[3], (KINDS, SCALES), jnp.float32, math.log(3.0), math.log(80.0))), 3.0, 80.0)
    scale_weight = jnp.clip(jax.random.uniform(arg_keys[4], (KINDS, SCALES), jnp.float32, 0.3, 1.0), 0.3, 1.0)
    return dict(control=control, scale_index=scale_index, length_x=length_x, length_y=length_y, scale_weight=scale_weight)


wind_gain = 2.0

def recursive_pass(values, inv_len, along, reverse):
    keep_rate = jnp.exp(-inv_len)
    weight = 1.0 - keep_rate
    leading = jnp.moveaxis(values, along, 0)

    def advance(running, column):
        running = keep_rate * running + weight * column
        return (running, running)
    initial = jnp.zeros(leading.shape[1:], jnp.float32)
    _, output = lax.scan(advance, initial, leading, reverse=reverse)
    return jnp.moveaxis(output, 0, along)

def filter_group(packed):
    values, inv_x, inv_y, amplitude = packed
    total = jnp.zeros_like(values)
    for scale in range(SCALES):
        smoothed = recursive_pass(values, inv_x[:, scale], 1, False)
        smoothed = recursive_pass(smoothed, inv_x[:, scale], 1, True)
        smoothed = recursive_pass(smoothed, inv_y[:, scale], 0, False)
        smoothed = recursive_pass(smoothed, inv_y[:, scale], 0, True)
        total = total + amplitude[:, scale] * smoothed
    return total

def reference(control, scale_index, length_x, length_y, scale_weight):
    along_x = length_x[scale_index]
    along_y = length_y[scale_index]
    chosen = scale_weight[scale_index]
    inv_x = 1.0 / along_x
    inv_y = 1.0 / along_y
    amplitude = 4.0 * chosen * jnp.sqrt(along_x * along_y)
    groups = SLABS // 8
    grouped = control.reshape(NY, NX, groups, 8).transpose(2, 0, 1, 3)
    filtered = lax.map(filter_group, (grouped, inv_x.reshape(groups, 8, SCALES), inv_y.reshape(groups, 8, SCALES), amplitude.reshape(groups, 8, SCALES)))
    increment = filtered.transpose(1, 2, 0, 3).reshape(NY, NX, SLABS)
    padded = jnp.pad(increment, ((1, 1), (1, 1), (0, 0)))
    north = padded[2:, 1:-1] - padded[:-2, 1:-1]
    east = padded[1:-1, 2:] - padded[1:-1, :-2]
    wind = jnp.stack([-wind_gain * north, wind_gain * east]).astype(jnp.bfloat16)
    return (increment, wind)
```

```python
import functools
import jax
import jax.numpy as jnp
from jax import lax
from jax.experimental import pallas as pl
from jax.experimental.pallas import tpu as pltpu
from jax.sharding import PartitionSpec as P

highest = lax.Precision.HIGHEST
group = 8
vmem_bytes = 56 * 1024 * 1024


def slab_coefficients(scale_index, length_x, length_y, scale_weight):
    kinds = length_x.shape[0]
    picks = (scale_index[:, None] == jnp.arange(kinds, dtype=jnp.int32)[None]).astype(jnp.float32)
    along_x = jnp.sum(picks[:, :, None] * length_x[None], axis=1)
    along_y = jnp.sum(picks[:, :, None] * length_y[None], axis=1)
    chosen = jnp.sum(picks[:, :, None] * scale_weight[None], axis=1)
    return (1.0 / along_x, 1.0 / along_y, 4.0 * chosen * jnp.sqrt(along_x * along_y))


def fwd_weight(is_fwd, src, dst, tile, inv):
    gap = jnp.maximum(dst - 1 - src, 0).astype(jnp.float32) * tile
    return jnp.where(is_fwd & (src < dst), jnp.exp(-gap * inv), 0.0)


def bwd_weight(is_fwd, src, dst, tile, tiles, inv):
    gap = jnp.maximum(src - dst - 1, 0).astype(jnp.float32) * tile
    fold = (1 + tile * (tiles - 1 - dst) + tile * (tiles - 1 - src)).astype(jnp.float32)
    return jnp.where(
        is_fwd, -jnp.exp(-fold * inv), jnp.where(src > dst, jnp.exp(-gap * inv), 0.0)
    )


def edge_weights(inv_x, tile):
    scales = inv_x.shape[1]
    j = jnp.arange(tile, dtype=jnp.float32)
    inv = inv_x[:, :, None]
    gain = 1.0 - jnp.exp(-inv)
    fwd = gain * jnp.exp(-(tile - 1.0 - j) * inv)
    bwd = gain * jnp.exp(-j * inv)
    pad = jnp.zeros((inv_x.shape[0], 8 - 2 * scales, tile), jnp.float32)
    return jnp.concatenate([fwd, bwd, pad], axis=1)


def carry_matrix(inv_x, tile, local, devices, me):
    scales = inv_x.shape[1]
    tiles = local * devices
    q = jnp.arange(tiles * 8, dtype=jnp.int32)[None, :, None]
    k = jnp.arange((local + 1) * 8, dtype=jnp.int32)[None, None, :]
    q_kind, q_tile = q % 8, q // 8
    k_kind, k_tile = k % 8, k // 8
    q_fwd = q_kind < scales
    k_fwd = k_kind < scales
    q_scale = q_kind - jnp.where(q_fwd, 0, scales)
    k_scale = k_kind - jnp.where(k_fwd, 0, scales)
    valid = (q_kind < 2 * scales) & (k_kind < 2 * scales) & (q_scale == k_scale)
    inv = inv_x[:, 0][:, None, None]
    for m in range(1, scales):
        inv = jnp.where(k_scale == m, inv_x[:, m][:, None, None], inv)
    r = jnp.exp(-inv)
    r_tile = jnp.exp(-inv * tile)
    first, last = me * local, me * local + local - 1
    inner = k_tile < local
    dst = jnp.where(inner, first + k_tile, jnp.where(k_fwd, first, last))
    c = fwd_weight(q_fwd, q_tile, dst, tile, inv)
    d = bwd_weight(q_fwd, q_tile, dst, tile, tiles, inv)
    own = q_tile == dst
    left = (c + r * (jnp.where(own & ~q_fwd, 1.0, 0.0) + r_tile * d)) / (1.0 + r)
    right = (r * (jnp.where(own & q_fwd, 1.0, 0.0) + r_tile * c) + d) / (1.0 + r)
    left = jnp.where(me == 0, 0.0, left)
    right = jnp.where(me == devices - 1, 0.0, right)
    value = jnp.where(inner, jnp.where(k_fwd, c, d), jnp.where(k_fwd, left, right))
    return jnp.where(valid, value, 0.0)


def split(value):
    high = value.astype(jnp.bfloat16)
    return high, (value - high.astype(jnp.float32)).astype(jnp.bfloat16)


def edge_kernel(tile, ctrl_ref, weight_ref, out_ref):
    rows, slabs, cols = ctrl_ref.shape
    for s in range(slabs):
        for t in range(cols // tile):
            piece = ctrl_ref[:, s, t * tile : (t + 1) * tile]
            out_ref[s, t * 8 : (t + 1) * 8, :] = lax.dot_general(
                weight_ref[s], piece, (((1,), (1,)), ((), ())),
                precision=highest, preferred_element_type=jnp.float32,
            )


def x_edges(ctrl, weights, tile):
    rows, slabs, cols = ctrl.shape
    local = cols // tile
    return pl.pallas_call(
        functools.partial(edge_kernel, tile),
        grid=(slabs // group,),
        in_specs=[
            pl.BlockSpec((rows, group, cols), lambda i: (0, i, 0)),
            pl.BlockSpec((group, 8, tile), lambda i: (i, 0, 0)),
        ],
        out_specs=pl.BlockSpec((group, local * 8, rows), lambda i: (i, 0, 0)),
        out_shape=jax.ShapeDtypeStruct((slabs, local * 8, rows), jnp.float32),
        compiler_params=pltpu.CompilerParams(vmem_limit_bytes=vmem_bytes),
        name="x_edges",
    )(ctrl, weights)


def x_kernel(tile, scales, ctrl_ref, gath_ref, carry_ref, inv_ref, ry_ref, w_ref, ye_ref):
    rows, slabs, cols = ctrl_ref.shape
    local = cols // tile
    width = w_ref.shape[3]
    lanes = scales * tile
    lane = lax.broadcasted_iota(jnp.int32, (tile, lanes), 1)
    row = lax.broadcasted_iota(jnp.int32, (tile, lanes), 0)
    scale_at = sum((lane >= m * tile).astype(jnp.int32) for m in range(1, scales))
    dist = jnp.abs(row - (lane - scale_at * tile)).astype(jnp.float32)
    one = lax.broadcasted_iota(jnp.int32, (1, lanes), 1)
    one_scale = sum((one >= m * tile).astype(jnp.int32) for m in range(1, scales))
    pos = (one - one_scale * tile).astype(jnp.float32)
    spot = lax.broadcasted_iota(jnp.int32, (rows, width - cols), 1)
    for s in range(slabs):
        inv = inv_ref[s]
        r = jnp.exp(-inv)
        high_k, low_k = split(jnp.exp(-dist * inv) * ((1.0 - r) / (1.0 + r)))
        from_left = jnp.exp(-(pos + 1.0) * inv) / (1.0 + r)
        from_right = jnp.exp(-(tile - pos) * inv) / (1.0 + r)
        gathered = jnp.concatenate([gath_ref[d, s] for d in range(gath_ref.shape[0])], axis=0)
        carry = lax.dot_general(
            gathered, carry_ref[s], (((0,), (0,)), ((), ())),
            precision=highest, preferred_element_type=jnp.float32,
        )
        for t in range(local):
            high, low = split(ctrl_ref[:, s, t * tile : (t + 1) * tile])
            dot = functools.partial(jnp.dot, preferred_element_type=jnp.float32)
            out = dot(high, high_k) + (dot(high, low_k) + dot(low, high_k))
            for m in range(scales):
                part = slice(m * tile, (m + 1) * tile)
                at = t * 8 + m
                w_ref[m, :, s, t * tile : (t + 1) * tile] = (
                    out[:, part]
                    + carry[:, at : at + 1] * from_left[:, part]
                    + carry[:, at + scales : at + scales + 1] * from_right[:, part]
                )
        for m in range(scales):
            at = local * 8 + m
            left = carry[:, at : at + 1]
            right = carry[:, at + scales : at + scales + 1]
            w_ref[m, :, s, cols:] = jnp.where(
                spot == 0, right, jnp.where(spot == width - cols - 1, left, 0.0)
            )

    owners = ye_ref.shape[0]
    each = slabs // owners
    zero = jnp.zeros((slabs, width), jnp.float32)
    rates = [ry_ref[m] for m in range(scales)]

    def widen(value):
        return jnp.concatenate([value] * (width // 128), axis=1)

    def step(y, state):
        fwd, bwd, power = state
        here = [w_ref[m, y] for m in range(scales)]
        fwd = tuple(widen(rates[m]) * fwd[m] + here[m] for m in range(scales))
        bwd = tuple(bwd[m] + widen(power[m]) * here[m] for m in range(scales))
        power = tuple(power[m] * rates[m] for m in range(scales))
        return fwd, bwd, power

    ones = jnp.ones((slabs, 128), jnp.float32)
    fwd, bwd, _ = lax.fori_loop(
        0, rows, step, ((zero,) * scales, (zero,) * scales, (ones,) * scales), unroll=4
    )
    for m in range(scales):
        for o in range(owners):
            mine = slice(o * each, (o + 1) * each)
            ye_ref[o, m * each : (m + 1) * each, :] = fwd[m][mine]
            ye_ref[o, (scales + m) * each : (scales + m + 1) * each, :] = bwd[m][mine]


def x_pass(ctrl, gathered, carry, inv_rows, rate_y, tile, width, subs):
    rows, slabs, cols = ctrl.shape
    scales = rate_y.shape[0]
    cols_n, _, edge_rows, _ = gathered.shape
    each = slabs // subs
    owners = group // each
    lanes = inv_rows.shape[2]
    return pl.pallas_call(
        functools.partial(x_kernel, tile, scales),
        grid=(slabs // group,),
        in_specs=[
            pl.BlockSpec((rows, group, cols), lambda i: (0, i, 0)),
            pl.BlockSpec((cols_n, group, edge_rows, rows), lambda i: (0, i, 0, 0)),
            pl.BlockSpec((group,) + carry.shape[1:], lambda i: (i, 0, 0)),
            pl.BlockSpec((group, 1, lanes), lambda i: (i, 0, 0)),
            pl.BlockSpec((scales, group, 128), lambda i: (0, i, 0)),
        ],
        out_specs=[
            pl.BlockSpec((scales, rows, group, width), lambda i: (0, 0, i, 0)),
            pl.BlockSpec((owners, 2 * scales * each, width), lambda i: (i, 0, 0)),
        ],
        out_shape=[
            jax.ShapeDtypeStruct((scales, rows, slabs, width), jnp.float32),
            jax.ShapeDtypeStruct((subs, 2 * scales * each, width), jnp.float32),
        ],
        compiler_params=pltpu.CompilerParams(vmem_limit_bytes=vmem_bytes),
        name="x_pass",
    )(ctrl, gathered, carry, inv_rows, rate_y)


def y_carries(arrived, inv_y, rows, subs, first_slab, each):
    scales = inv_y.shape[1]
    width = arrived.shape[2]
    inv = lax.dynamic_slice_in_dim(inv_y, first_slab, each, 0).T.reshape(scales * each)
    src = jnp.arange(subs, dtype=jnp.int32)[None, :, None]
    dst = jnp.arange(subs, dtype=jnp.int32)[:, None, None]
    inv = inv[None, None, :]
    r = jnp.exp(-inv)
    r_tile = jnp.exp(-inv * rows)
    parts = []
    for is_fwd in (True, False):
        flag = jnp.full((1, 1, 1), is_fwd)
        c = fwd_weight(flag, src, dst, rows, inv)
        d = bwd_weight(flag, src, dst, rows, subs, inv)
        own = jnp.where((src == dst) & flag, 1.0, 0.0)
        right = (r * (own + r_tile * c) + d) / ((1.0 + r) * (1.0 - r))
        right = jnp.where(dst == subs - 1, 0.0, right)
        parts.append(jnp.concatenate([c, right], axis=2))
    half = scales * each
    total = 0.0
    for a in range(subs):
        fwd = jnp.concatenate([arrived[a, :half]] * 2, axis=0)
        bwd = jnp.concatenate([arrived[a, half:]] * 2, axis=0)
        total = total + parts[0][:, a, :, None] * fwd[None] + parts[1][:, a, :, None] * bwd[None]
    return total


def y_kernel(scales, first_ref, w_ref, carry_ref, par_ref, inc_ref, wind_ref, held):
    _, rows, slabs, width = w_ref.shape
    cols = inc_ref.shape[2]

    def widen(value):
        return jnp.concatenate([value] * (width // 128), axis=1)

    rates = [par_ref[m] for m in range(scales)]
    gains = [par_ref[scales + m] for m in range(scales)]
    start = tuple(carry_ref[m] for m in range(scales))

    def ahead(y, state):
        state = tuple(widen(rates[m]) * state[m] + w_ref[m, y] for m in range(scales))
        for m in range(scales):
            held[m, y] = state[m]
        return state

    lax.fori_loop(0, rows, ahead, start, unroll=2)
    ends = tuple(carry_ref[scales + m] for m in range(scales))

    def mix(state):
        return sum(widen(gains[m]) * state[m] for m in range(scales))

    def back(i, carried):
        y = rows - 1 - i
        state, after, later = carried
        state = tuple(widen(rates[m]) * state[m] + held[m, y] for m in range(scales))
        total = mix(state)
        here = total[:, :cols]
        inc_ref[y] = here
        east = pltpu.roll(total, width - 1, 1)[:, :cols] - pltpu.roll(total, 1, 1)[:, :cols]
        wind_ref[1, y] = (2.0 * east).astype(jnp.bfloat16)

        @pl.when(i > 0)
        def _():
            wind_ref[0, y + 1] = (-2.0 * (later - here)).astype(jnp.bfloat16)

        return state, here, after

    below = mix(ends)[:, :cols]
    state, after, later = lax.fori_loop(0, rows, back, (ends, below, below), unroll=2)
    above = mix(tuple(widen(rates[m]) * state[m] + start[m] for m in range(scales)))[:, :cols]
    above = jnp.where(first_ref[0] == 1, 0.0, above)
    wind_ref[0, 0] = (-2.0 * (later - above)).astype(jnp.bfloat16)


def y_pass(first, smoothed, carries, params, cols):
    scales, rows, slabs, width = smoothed.shape
    block = 16
    return pl.pallas_call(
        functools.partial(y_kernel, scales),
        grid=(slabs // block,),
        in_specs=[
            pl.BlockSpec(memory_space=pltpu.SMEM),
            pl.BlockSpec((scales, rows, block, width), lambda i: (0, 0, i, 0)),
            pl.BlockSpec((2 * scales, block, width), lambda i: (0, i, 0)),
            pl.BlockSpec((2 * scales, block, 128), lambda i: (0, i, 0)),
        ],
        out_specs=[
            pl.BlockSpec((rows, block, cols), lambda i: (0, i, 0)),
            pl.BlockSpec((2, rows, block, cols), lambda i: (0, 0, i, 0)),
        ],
        out_shape=[
            jax.ShapeDtypeStruct((rows, slabs, cols), jnp.float32),
            jax.ShapeDtypeStruct((2, rows, slabs, cols), jnp.bfloat16),
        ],
        scratch_shapes=[pltpu.VMEM((scales, rows, block, width), jnp.float32)],
        compiler_params=pltpu.CompilerParams(vmem_limit_bytes=vmem_bytes),
        name="y_pass",
    )(first, smoothed, carries, params)


def per_device(control, scale_index, length_x, length_y, scale_weight):
    inv_x, inv_y, amplitude = slab_coefficients(scale_index, length_x, length_y, scale_weight)
    subs, cols_n = lax.axis_size("sub"), lax.axis_size("col")
    rows, cols, slabs = control.shape
    scales = inv_x.shape[1]
    tile = 128 if cols % 128 == 0 else cols
    local = cols // tile
    width = (cols // 128 + 1) * 128
    each = slabs // subs
    me = lax.axis_index("sub")
    ctrl = control.transpose(0, 2, 1)
    edges = x_edges(ctrl, edge_weights(inv_x, tile), tile)
    gathered = lax.all_gather(edges, "col")
    carry = carry_matrix(inv_x, tile, local, cols_n, lax.axis_index("col"))
    inv_rows = jnp.repeat(inv_x, tile, axis=1)[:, None, :]
    rate = jnp.exp(-inv_y)
    rate_y = jnp.broadcast_to(rate.T[:, :, None], (scales, slabs, 128))
    smoothed, y_edges = x_pass(ctrl, gathered, carry, inv_rows, rate_y, tile, width, subs)
    arrived = lax.all_to_all(y_edges, "sub", split_axis=0, concat_axis=0, tiled=True)
    summed = y_carries(arrived, inv_y, rows, subs, me * each, each)
    returned = lax.all_to_all(summed, "sub", split_axis=0, concat_axis=0, tiled=True)
    carries = returned.reshape(subs, 2 * scales, each, width).transpose(1, 0, 2, 3)
    carries = carries.reshape(2 * scales, slabs, width)
    gain = (amplitude * (1.0 - rate) * (1.0 - rate)).T
    gain = jnp.broadcast_to(gain[:, :, None], (scales, slabs, 128))
    params = jnp.concatenate([rate_y, gain], axis=0)
    first = (me == 0).astype(jnp.int32)[None]
    increment, wind = y_pass(first, smoothed, carries, params, cols)
    return (increment.transpose(0, 2, 1), wind.transpose(0, 1, 3, 2))


def solution(mesh):
    placed = (P("sub", "col", None), P(), P(), P(), P())
    return jax.shard_map(
        per_device,
        mesh=mesh,
        in_specs=placed,
        out_specs=(P("sub", "col", None), P(None, "sub", "col", None)),
        check_vma=False,
    )
```

```python
import functools
import jax
import jax.numpy as jnp
from jax import lax
from jax.experimental import pallas as pl
from jax.experimental.pallas import tpu as pltpu
from jax.sharding import PartitionSpec as P

group = 8
vmem_bytes = 56 * 1024 * 1024


def slab_coefficients(scale_index, length_x, length_y, scale_weight):
    kinds = length_x.shape[0]
    picks = (scale_index[:, None] == jnp.arange(kinds, dtype=jnp.int32)[None]).astype(jnp.float32)
    along_x = jnp.sum(picks[:, :, None] * length_x[None], axis=1)
    along_y = jnp.sum(picks[:, :, None] * length_y[None], axis=1)
    chosen = jnp.sum(picks[:, :, None] * scale_weight[None], axis=1)
    return (1.0 / along_x, 1.0 / along_y, 4.0 * chosen * jnp.sqrt(along_x * along_y))


def fwd_weight(is_fwd, src, dst, tile, inv):
    gap = jnp.maximum(dst - 1 - src, 0).astype(jnp.float32) * tile
    return jnp.where(is_fwd & (src < dst), jnp.exp(-gap * inv), 0.0)


def bwd_weight(is_fwd, src, dst, tile, tiles, inv):
    gap = jnp.maximum(src - dst - 1, 0).astype(jnp.float32) * tile
    fold = (1 + tile * (tiles - 1 - dst) + tile * (tiles - 1 - src)).astype(jnp.float32)
    return jnp.where(
        is_fwd, -jnp.exp(-fold * inv), jnp.where(src > dst, jnp.exp(-gap * inv), 0.0)
    )


def edge_weights(inv_x, tile):
    scales = inv_x.shape[1]
    j = jnp.arange(tile, dtype=jnp.float32)
    inv = inv_x[:, :, None]
    gain = 1.0 - jnp.exp(-inv)
    fwd = gain * jnp.exp(-(tile - 1.0 - j) * inv)
    bwd = gain * jnp.exp(-j * inv)
    pad = jnp.zeros((inv_x.shape[0], 8 - 2 * scales, tile), jnp.float32)
    return jnp.concatenate([fwd, bwd, pad], axis=1)


def carry_matrix(inv_x, tile, local, devices, me):
    scales = inv_x.shape[1]
    tiles = local * devices
    q = jnp.arange(tiles * 8, dtype=jnp.int32)[None, :, None]
    k = jnp.arange((local + 1) * 8, dtype=jnp.int32)[None, None, :]
    q_kind, q_tile = q % 8, q // 8
    k_kind, k_tile = k % 8, k // 8
    q_fwd = q_kind < scales
    k_fwd = k_kind < scales
    q_scale = q_kind - jnp.where(q_fwd, 0, scales)
    k_scale = k_kind - jnp.where(k_fwd, 0, scales)
    valid = (q_kind < 2 * scales) & (k_kind < 2 * scales) & (q_scale == k_scale)
    inv = inv_x[:, 0][:, None, None]
    for m in range(1, scales):
        inv = jnp.where(k_scale == m, inv_x[:, m][:, None, None], inv)
    r = jnp.exp(-inv)
    r_tile = jnp.exp(-inv * tile)
    first, last = me * local, me * local + local - 1
    inner = k_tile < local
    dst = jnp.where(inner, first + k_tile, jnp.where(k_fwd, first, last))
    c = fwd_weight(q_fwd, q_tile, dst, tile, inv)
    d = bwd_weight(q_fwd, q_tile, dst, tile, tiles, inv)
    own = q_tile == dst
    left = (c + r * (jnp.where(own & ~q_fwd, 1.0, 0.0) + r_tile * d)) / (1.0 + r)
    right = (r * (jnp.where(own & q_fwd, 1.0, 0.0) + r_tile * c) + d) / (1.0 + r)
    left = jnp.where(me == 0, 0.0, left)
    right = jnp.where(me == devices - 1, 0.0, right)
    value = jnp.where(inner, jnp.where(k_fwd, c, d), jnp.where(k_fwd, left, right))
    return jnp.where(valid, value, 0.0)


def split(value):
    high = value.astype(jnp.bfloat16)
    return high, (value - high.astype(jnp.float32)).astype(jnp.bfloat16)


def split_weights(value):
    high, low = split(value)
    top = jnp.concatenate([high, low], axis=1)
    return jnp.concatenate([top, jnp.concatenate([high, jnp.zeros_like(low)], axis=1)], axis=0)


def stacked_tiles(ctrl_ref, s, tile):
    cols = ctrl_ref.shape[2]
    pieces = [ctrl_ref[:, s, t * tile : (t + 1) * tile] for t in range(cols // tile)]
    return jnp.concatenate(split(jnp.concatenate(pieces, axis=0)), axis=1)


def edge_kernel(tile, ctrl_ref, weight_ref, out_ref):
    rows, slabs, cols = ctrl_ref.shape
    for s in range(slabs):
        out = jnp.dot(
            stacked_tiles(ctrl_ref, s, tile),
            split_weights(weight_ref[s]),
            preferred_element_type=jnp.float32,
        )
        out = out[:, :8] + out[:, 8:16]
        for t in range(cols // tile):
            out_ref[s, t * 8 : (t + 1) * 8, :] = out[t * rows : (t + 1) * rows].T


def x_edges(ctrl, weights, tile):
    rows, slabs, cols = ctrl.shape
    local = cols // tile
    return pl.pallas_call(
        functools.partial(edge_kernel, tile),
        grid=(slabs // group,),
        in_specs=[
            pl.BlockSpec((rows, group, cols), lambda i: (0, i, 0)),
            pl.BlockSpec((group, tile, 8), lambda i: (i, 0, 0)),
        ],
        out_specs=pl.BlockSpec((group, local * 8, rows), lambda i: (i, 0, 0)),
        out_shape=jax.ShapeDtypeStruct((slabs, local * 8, rows), jnp.float32),
        compiler_params=pltpu.CompilerParams(vmem_limit_bytes=vmem_bytes),
        name="x_edges",
    )(ctrl, weights)


def x_kernel(tile, scales, ctrl_ref, gath_ref, carry_ref, inv_ref, ry_ref, w_ref, ye_ref):
    rows, slabs, cols = ctrl_ref.shape
    local = cols // tile
    width = w_ref.shape[3]
    lanes = scales * tile
    lane = lax.broadcasted_iota(jnp.int32, (tile, lanes), 1)
    row = lax.broadcasted_iota(jnp.int32, (tile, lanes), 0)
    scale_at = sum((lane >= m * tile).astype(jnp.int32) for m in range(1, scales))
    dist = jnp.abs(row - (lane - scale_at * tile)).astype(jnp.float32)
    one = lax.broadcasted_iota(jnp.int32, (1, lanes), 1)
    one_scale = sum((one >= m * tile).astype(jnp.int32) for m in range(1, scales))
    pos = (one - one_scale * tile).astype(jnp.float32)
    spot = lax.broadcasted_iota(jnp.int32, (rows, width - cols), 1)
    for s in range(slabs):
        inv = inv_ref[s]
        r = jnp.exp(-inv)
        weights = split_weights(jnp.exp(-dist * inv) * ((1.0 - r) / (1.0 + r)))
        from_left = jnp.exp(-(pos + 1.0) * inv) / (1.0 + r)
        from_right = jnp.exp(-(tile - pos) * inv) / (1.0 + r)
        gathered = jnp.concatenate([gath_ref[d, s] for d in range(gath_ref.shape[0])], axis=0)
        carry = lax.dot_general(
            jnp.concatenate(split(gathered), axis=0), split_weights(carry_ref[s]),
            (((0,), (0,)), ((), ())), preferred_element_type=jnp.float32,
        )
        kinds = carry.shape[1] // 2
        carry = carry[:, :kinds] + carry[:, kinds:]
        whole = jnp.dot(
            stacked_tiles(ctrl_ref, s, tile), weights, preferred_element_type=jnp.float32
        )
        for t in range(local):
            out = whole[t * rows : (t + 1) * rows]
            out = out[:, :lanes] + out[:, lanes:]
            for m in range(scales):
                part = slice(m * tile, (m + 1) * tile)
                at = t * 8 + m
                w_ref[m, :, s, t * tile : (t + 1) * tile] = (
                    out[:, part]
                    + carry[:, at : at + 1] * from_left[:, part]
                    + carry[:, at + scales : at + scales + 1] * from_right[:, part]
                )
        for m in range(scales):
            at = local * 8 + m
            left = carry[:, at : at + 1]
            right = carry[:, at + scales : at + scales + 1]
            w_ref[m, :, s, cols:] = jnp.where(
                spot == 0, right, jnp.where(spot == width - cols - 1, left, 0.0)
            )

    owners = ye_ref.shape[0]
    each = slabs // owners
    zero = jnp.zeros((slabs, width), jnp.float32)
    rates = [ry_ref[m] for m in range(scales)]

    def widen(value):
        return jnp.concatenate([value] * (width // 128), axis=1)

    def step(y, state):
        fwd, bwd, power = state
        here = [w_ref[m, y] for m in range(scales)]
        fwd = tuple(widen(rates[m]) * fwd[m] + here[m] for m in range(scales))
        bwd = tuple(bwd[m] + widen(power[m]) * here[m] for m in range(scales))
        power = tuple(power[m] * rates[m] for m in range(scales))
        return fwd, bwd, power

    ones = jnp.ones((slabs, 128), jnp.float32)
    fwd, bwd, _ = lax.fori_loop(
        0, rows, step, ((zero,) * scales, (zero,) * scales, (ones,) * scales), unroll=4
    )
    for m in range(scales):
        for o in range(owners):
            mine = slice(o * each, (o + 1) * each)
            ye_ref[o, m * each : (m + 1) * each, :] = fwd[m][mine]
            ye_ref[o, (scales + m) * each : (scales + m + 1) * each, :] = bwd[m][mine]


def x_pass(ctrl, gathered, carry, inv_rows, rate_y, tile, width, subs):
    rows, slabs, cols = ctrl.shape
    scales = rate_y.shape[0]
    cols_n, _, edge_rows, _ = gathered.shape
    each = slabs // subs
    owners = group // each
    lanes = inv_rows.shape[2]
    return pl.pallas_call(
        functools.partial(x_kernel, tile, scales),
        grid=(slabs // group,),
        in_specs=[
            pl.BlockSpec((rows, group, cols), lambda i: (0, i, 0)),
            pl.BlockSpec((cols_n, group, edge_rows, rows), lambda i: (0, i, 0, 0)),
            pl.BlockSpec((group,) + carry.shape[1:], lambda i: (i, 0, 0)),
            pl.BlockSpec((group, 1, lanes), lambda i: (i, 0, 0)),
            pl.BlockSpec((scales, group, 128), lambda i: (0, i, 0)),
        ],
        out_specs=[
            pl.BlockSpec((scales, rows, group, width), lambda i: (0, 0, i, 0)),
            pl.BlockSpec((owners, 2 * scales * each, width), lambda i: (i, 0, 0)),
        ],
        out_shape=[
            jax.ShapeDtypeStruct((scales, rows, slabs, width), jnp.float32),
            jax.ShapeDtypeStruct((subs, 2 * scales * each, width), jnp.float32),
        ],
        compiler_params=pltpu.CompilerParams(vmem_limit_bytes=vmem_bytes),
        name="x_pass",
    )(ctrl, gathered, carry, inv_rows, rate_y)


def greet(axis, size):
    me = lax.axis_index(axis)
    barrier = pltpu.get_barrier_semaphore()
    for k in range(1, size):
        pl.semaphore_signal(
            barrier, inc=1, device_id={axis: lax.rem(me + k, size)},
            device_id_type=pl.DeviceIdType.MESH,
        )
    pl.semaphore_wait(barrier, size - 1)


def send_all(axis, size, source, target, send_sems, recv_sems):
    me = lax.axis_index(axis)
    copies = []
    for k in range(1, size):
        partner = lax.rem(me + k, size)
        copies.append(
            pltpu.make_async_remote_copy(
                src_ref=source(partner), dst_ref=target.at[me],
                send_sem=send_sems.at[k], recv_sem=recv_sems.at[k],
                device_id={axis: partner}, device_id_type=pl.DeviceIdType.MESH,
            )
        )
        copies[-1].start()
    return copies


def gather_kernel(axis, size, own_ref, all_ref, send_sems, recv_sems):
    greet(axis, size)
    copies = send_all(axis, size, lambda p: own_ref, all_ref, send_sems, recv_sems)
    all_ref[lax.axis_index(axis)] = own_ref[...]
    for copy in copies:
        copy.wait()


def gather(own, axis):
    size = lax.axis_size(axis)
    vmem = pl.BlockSpec(memory_space=pltpu.VMEM)
    return pl.pallas_call(
        functools.partial(gather_kernel, axis, size),
        in_specs=[vmem],
        out_specs=vmem,
        out_shape=jax.ShapeDtypeStruct((size,) + own.shape, own.dtype),
        scratch_shapes=[pltpu.SemaphoreType.DMA((size,)), pltpu.SemaphoreType.DMA((size,))],
        compiler_params=pltpu.CompilerParams(
            collective_id=0, has_side_effects=True, vmem_limit_bytes=vmem_bytes
        ),
        name="x_gather",
    )(own)


def y_exchange_kernel(axis, size, edge_ref, rate_ref, out_ref, arrived, summed, *sems):
    me = lax.axis_index(axis)
    greet(axis, size)
    copies = send_all(axis, size, lambda p: edge_ref.at[p], arrived, sems[0], sems[1])
    arrived[me] = edge_ref[me]
    for copy in copies:
        copy.wait()
    half = edge_ref.shape[1] // 2
    width = edge_ref.shape[2]
    r, r_band, gain = [
        jnp.concatenate([rate_ref[k]] * (width // 128), axis=1) for k in range(3)
    ]
    value = jnp.zeros((half, width), jnp.float32)
    for a in range(size):
        summed[a, :half, :] = value
        value = r_band * value + arrived[a, :half, :]
    back = -r * value
    summed[size - 1, half:, :] = jnp.zeros((half, width), jnp.float32)
    for a in range(size - 1, 0, -1):
        back = r_band * back + arrived[a, half:, :]
        summed[a - 1, half:, :] = (r * summed[a, :half, :] + back) * gain
    copies = send_all(axis, size, lambda p: summed.at[p], out_ref, sems[2], sems[3])
    out_ref[me] = summed[me]
    for copy in copies:
        copy.wait()


def y_exchange(y_edges, inv, rows, axis):
    size = lax.axis_size(axis)
    r = jnp.exp(-inv)
    rates = jnp.stack([r, jnp.exp(-inv * rows), 1.0 / ((1.0 + r) * (1.0 - r))])
    rates = jnp.broadcast_to(rates[:, :, None], rates.shape + (128,))
    vmem = pl.BlockSpec(memory_space=pltpu.VMEM)
    shape = y_edges.shape
    return pl.pallas_call(
        functools.partial(y_exchange_kernel, axis, size),
        in_specs=[vmem] * 2,
        out_specs=vmem,
        out_shape=jax.ShapeDtypeStruct(shape, jnp.float32),
        scratch_shapes=[pltpu.VMEM(shape, jnp.float32)] * 2
        + [pltpu.SemaphoreType.DMA((size,))] * 4,
        compiler_params=pltpu.CompilerParams(
            collective_id=1, has_side_effects=True, vmem_limit_bytes=vmem_bytes
        ),
        name="y_exchange",
    )(y_edges, rates)


def y_kernel(scales, first_ref, w_ref, carry_ref, par_ref, inc_ref, wind_ref, held):
    _, rows, slabs, width = w_ref.shape
    cols = inc_ref.shape[2]

    def widen(value):
        return jnp.concatenate([value] * (width // 128), axis=1)

    rates = [par_ref[m] for m in range(scales)]
    gains = [par_ref[scales + m] for m in range(scales)]
    start = tuple(carry_ref[m] for m in range(scales))

    def ahead(y, state):
        state = tuple(widen(rates[m]) * state[m] + w_ref[m, y] for m in range(scales))
        for m in range(scales):
            held[m, y] = state[m]
        return state

    lax.fori_loop(0, rows, ahead, start, unroll=4)
    ends = tuple(carry_ref[scales + m] for m in range(scales))

    def mix(state):
        return sum(widen(gains[m]) * state[m] for m in range(scales))

    def back(i, state):
        y = rows - 1 - i
        state = tuple(widen(rates[m]) * state[m] + held[m, y] for m in range(scales))
        total = mix(state)
        here = total[:, :cols]
        inc_ref[y] = here
        east = pltpu.roll(total, width - 1, 1)[:, :cols] - pltpu.roll(total, 1, 1)[:, :cols]
        wind_ref[1, y] = (2.0 * east).astype(jnp.bfloat16)
        return state

    state = lax.fori_loop(0, rows, back, ends, unroll=4)
    below = mix(ends)[:, :cols]
    above = mix(tuple(widen(rates[m]) * state[m] + start[m] for m in range(scales)))[:, :cols]
    above = jnp.where(first_ref[0] == 1, 0.0, above)
    wind_ref[0, 0] = (-2.0 * (inc_ref[1] - above)).astype(jnp.bfloat16)
    wind_ref[0, rows - 1] = (-2.0 * (below - inc_ref[rows - 2])).astype(jnp.bfloat16)

    def north(y, _):
        wind_ref[0, y] = (-2.0 * (inc_ref[y + 1] - inc_ref[y - 1])).astype(jnp.bfloat16)
        return _

    lax.fori_loop(1, rows - 1, north, 0, unroll=2)


def y_pass(first, smoothed, carries, params, cols):
    scales, rows, slabs, width = smoothed.shape
    block = 16
    return pl.pallas_call(
        functools.partial(y_kernel, scales),
        grid=(slabs // block,),
        in_specs=[
            pl.BlockSpec(memory_space=pltpu.SMEM),
            pl.BlockSpec((scales, rows, block, width), lambda i: (0, 0, i, 0)),
            pl.BlockSpec((2 * scales, block, width), lambda i: (0, i, 0)),
            pl.BlockSpec((2 * scales, block, 128), lambda i: (0, i, 0)),
        ],
        out_specs=[
            pl.BlockSpec((rows, block, cols), lambda i: (0, i, 0)),
            pl.BlockSpec((2, rows, block, cols), lambda i: (0, 0, i, 0)),
        ],
        out_shape=[
            jax.ShapeDtypeStruct((rows, slabs, cols), jnp.float32),
            jax.ShapeDtypeStruct((2, rows, slabs, cols), jnp.bfloat16),
        ],
        scratch_shapes=[pltpu.VMEM((scales, rows, block, width), jnp.float32)],
        compiler_params=pltpu.CompilerParams(vmem_limit_bytes=vmem_bytes),
        name="y_pass",
    )(first, smoothed, carries, params)


def per_device(control, scale_index, length_x, length_y, scale_weight):
    inv_x, inv_y, amplitude = slab_coefficients(scale_index, length_x, length_y, scale_weight)
    subs, cols_n = lax.axis_size("sub"), lax.axis_size("col")
    rows, cols, slabs = control.shape
    scales = inv_x.shape[1]
    tile = 128 if cols % 128 == 0 else cols
    local = cols // tile
    width = (cols // 128 + 1) * 128
    each = slabs // subs
    me = lax.axis_index("sub")
    ctrl = control.transpose(0, 2, 1)
    edges = x_edges(ctrl, edge_weights(inv_x, tile).transpose(0, 2, 1), tile)
    gathered = gather(edges, "col")
    carry = carry_matrix(inv_x, tile, local, cols_n, lax.axis_index("col"))
    inv_rows = jnp.repeat(inv_x, tile, axis=1)[:, None, :]
    rate = jnp.exp(-inv_y)
    rate_y = jnp.broadcast_to(rate.T[:, :, None], (scales, slabs, 128))
    smoothed, y_edges = x_pass(ctrl, gathered, carry, inv_rows, rate_y, tile, width, subs)
    owned = lax.dynamic_slice_in_dim(inv_y, me * each, each, 0).T.reshape(scales * each)
    returned = y_exchange(y_edges, owned, rows, "sub")
    carries = returned.reshape(subs, 2 * scales, each, width).transpose(1, 0, 2, 3)
    carries = carries.reshape(2 * scales, slabs, width)
    gain = (amplitude * (1.0 - rate) * (1.0 - rate)).T
    gain = jnp.broadcast_to(gain[:, :, None], (scales, slabs, 128))
    params = jnp.concatenate([rate_y, gain], axis=0)
    first = (me == 0).astype(jnp.int32)[None]
    increment, wind = y_pass(first, smoothed, carries, params, cols)
    return (increment.transpose(0, 2, 1), wind.transpose(0, 1, 3, 2))


def solution(mesh):
    placed = (P("sub", "col", None), P(), P(), P(), P())
    return jax.shard_map(
        per_device,
        mesh=mesh,
        in_specs=placed,
        out_specs=(P("sub", "col", None), P(None, "sub", "col", None)),
        check_vma=False,
    )
```

```python
import functools
import jax
import jax.numpy as jnp
from jax import lax
from jax.experimental import pallas as pl
from jax.experimental.pallas import tpu as pltpu
from jax.sharding import PartitionSpec as P

group = 8
vmem_bytes = 56 * 1024 * 1024


def slab_coefficients(scale_index, length_x, length_y, scale_weight):
    kinds = length_x.shape[0]
    picks = (scale_index[:, None] == jnp.arange(kinds, dtype=jnp.int32)[None]).astype(jnp.float32)
    along_x = jnp.sum(picks[:, :, None] * length_x[None], axis=1)
    along_y = jnp.sum(picks[:, :, None] * length_y[None], axis=1)
    chosen = jnp.sum(picks[:, :, None] * scale_weight[None], axis=1)
    return (1.0 / along_x, 1.0 / along_y, 4.0 * chosen * jnp.sqrt(along_x * along_y))


def fwd_weight(is_fwd, src, dst, tile, inv):
    gap = jnp.maximum(dst - 1 - src, 0).astype(jnp.float32) * tile
    return jnp.where(is_fwd & (src < dst), jnp.exp(-gap * inv), 0.0)


def bwd_weight(is_fwd, src, dst, tile, tiles, inv):
    gap = jnp.maximum(src - dst - 1, 0).astype(jnp.float32) * tile
    fold = (1 + tile * (tiles - 1 - dst) + tile * (tiles - 1 - src)).astype(jnp.float32)
    return jnp.where(
        is_fwd, -jnp.exp(-fold * inv), jnp.where(src > dst, jnp.exp(-gap * inv), 0.0)
    )


def edge_weights(inv_x, tile):
    scales = inv_x.shape[1]
    j = jnp.arange(tile, dtype=jnp.float32)
    inv = inv_x[:, :, None]
    gain = 1.0 - jnp.exp(-inv)
    fwd = gain * jnp.exp(-(tile - 1.0 - j) * inv)
    bwd = gain * jnp.exp(-j * inv)
    pad = jnp.zeros((inv_x.shape[0], 8 - 2 * scales, tile), jnp.float32)
    return jnp.concatenate([fwd, bwd, pad], axis=1)


def carry_matrix(inv_x, tile, local, devices, me):
    scales = inv_x.shape[1]
    tiles = local * devices
    q = jnp.arange(tiles * 8, dtype=jnp.int32)[None, :, None]
    k = jnp.arange((local + 1) * 8, dtype=jnp.int32)[None, None, :]
    q_kind, q_tile = q % 8, q // 8
    k_kind, k_tile = k % 8, k // 8
    q_fwd = q_kind < scales
    k_fwd = k_kind < scales
    q_scale = q_kind - jnp.where(q_fwd, 0, scales)
    k_scale = k_kind - jnp.where(k_fwd, 0, scales)
    valid = (q_kind < 2 * scales) & (k_kind < 2 * scales) & (q_scale == k_scale)
    inv = inv_x[:, 0][:, None, None]
    for m in range(1, scales):
        inv = jnp.where(k_scale == m, inv_x[:, m][:, None, None], inv)
    r = jnp.exp(-inv)
    r_tile = jnp.exp(-inv * tile)
    first, last = me * local, me * local + local - 1
    inner = k_tile < local
    dst = jnp.where(inner, first + k_tile, jnp.where(k_fwd, first, last))
    c = fwd_weight(q_fwd, q_tile, dst, tile, inv)
    d = bwd_weight(q_fwd, q_tile, dst, tile, tiles, inv)
    own = q_tile == dst
    left = (c + r * (jnp.where(own & ~q_fwd, 1.0, 0.0) + r_tile * d)) / (1.0 + r)
    right = (r * (jnp.where(own & q_fwd, 1.0, 0.0) + r_tile * c) + d) / (1.0 + r)
    left = jnp.where(me == 0, 0.0, left)
    right = jnp.where(me == devices - 1, 0.0, right)
    value = jnp.where(inner, jnp.where(k_fwd, c, d), jnp.where(k_fwd, left, right))
    return jnp.where(valid, value, 0.0)


def split(value):
    high = value.astype(jnp.bfloat16)
    return high, (value - high.astype(jnp.float32)).astype(jnp.bfloat16)


def split_weights(value):
    high, low = split(value)
    top = jnp.concatenate([high, low], axis=1)
    return jnp.concatenate([top, jnp.concatenate([high, jnp.zeros_like(low)], axis=1)], axis=0)


def stacked_tiles(ctrl_ref, s, tile):
    cols = ctrl_ref.shape[2]
    pieces = [ctrl_ref[:, s, t * tile : (t + 1) * tile] for t in range(cols // tile)]
    return jnp.concatenate(split(jnp.concatenate(pieces, axis=0)), axis=1)


def edge_kernel(tile, ctrl_ref, weight_ref, out_ref):
    rows, slabs, cols = ctrl_ref.shape
    for s in range(slabs):
        out = jnp.dot(
            stacked_tiles(ctrl_ref, s, tile),
            split_weights(weight_ref[s]),
            preferred_element_type=jnp.float32,
        )
        out = out[:, :8] + out[:, 8:16]
        for t in range(cols // tile):
            out_ref[s, t * 8 : (t + 1) * 8, :] = out[t * rows : (t + 1) * rows].T


def x_edges(ctrl, weights, tile):
    rows, slabs, cols = ctrl.shape
    local = cols // tile
    return pl.pallas_call(
        functools.partial(edge_kernel, tile),
        grid=(slabs // group,),
        in_specs=[
            pl.BlockSpec((rows, group, cols), lambda i: (0, i, 0)),
            pl.BlockSpec((group, tile, 8), lambda i: (i, 0, 0)),
        ],
        out_specs=pl.BlockSpec((group, local * 8, rows), lambda i: (i, 0, 0)),
        out_shape=jax.ShapeDtypeStruct((slabs, local * 8, rows), jnp.float32),
        compiler_params=pltpu.CompilerParams(vmem_limit_bytes=vmem_bytes),
        name="x_edges",
    )(ctrl, weights)


def x_kernel(tile, scales, ctrl_ref, gath_ref, carry_ref, inv_ref, ry_ref, w_ref, ye_ref, held):
    rows, slabs, cols = ctrl_ref.shape
    local = cols // tile
    width = w_ref.shape[3]
    lanes = scales * tile
    lane = lax.broadcasted_iota(jnp.int32, (tile, lanes), 1)
    row = lax.broadcasted_iota(jnp.int32, (tile, lanes), 0)
    scale_at = sum((lane >= m * tile).astype(jnp.int32) for m in range(1, scales))
    dist = jnp.abs(row - (lane - scale_at * tile)).astype(jnp.float32)
    one = lax.broadcasted_iota(jnp.int32, (1, lanes), 1)
    one_scale = sum((one >= m * tile).astype(jnp.int32) for m in range(1, scales))
    pos = (one - one_scale * tile).astype(jnp.float32)
    spot = lax.broadcasted_iota(jnp.int32, (rows, width - cols), 1)

    def put(m, s, start, stop, value):
        if tile != 128:
            w_ref[m, :, s, start:stop] = value
            return
        held[m, s, :, start:stop] = value

    for s in range(slabs):
        inv = inv_ref[s]
        r = jnp.exp(-inv)
        weights = split_weights(jnp.exp(-dist * inv) * ((1.0 - r) / (1.0 + r)))
        from_left = jnp.exp(-(pos + 1.0) * inv) / (1.0 + r)
        from_right = jnp.exp(-(tile - pos) * inv) / (1.0 + r)
        gathered = jnp.concatenate([gath_ref[d, s] for d in range(gath_ref.shape[0])], axis=0)
        carry = lax.dot_general(
            jnp.concatenate(split(gathered), axis=0), split_weights(carry_ref[s]),
            (((0,), (0,)), ((), ())), preferred_element_type=jnp.float32,
        )
        kinds = carry.shape[1] // 2
        carry = carry[:, :kinds] + carry[:, kinds:]
        whole = jnp.dot(
            stacked_tiles(ctrl_ref, s, tile), weights, preferred_element_type=jnp.float32
        )
        for t in range(local):
            out = whole[t * rows : (t + 1) * rows]
            out = out[:, :lanes] + out[:, lanes:]
            for m in range(scales):
                part = slice(m * tile, (m + 1) * tile)
                at = t * 8 + m
                put(m, s, t * tile, (t + 1) * tile, (
                    out[:, part]
                    + carry[:, at : at + 1] * from_left[:, part]
                    + carry[:, at + scales : at + scales + 1] * from_right[:, part]
                ))
        for m in range(scales):
            at = local * 8 + m
            left = carry[:, at : at + 1]
            right = carry[:, at + scales : at + scales + 1]
            halo = jnp.where(spot == 0, right, jnp.where(spot == width - cols - 1, left, 0.0))
            put(m, s, cols, width, halo)

    if tile == 128:
        for m in range(scales):
            for at in range(0, width, 128):
                w_ref[m, :, :, at : at + 128] = jnp.swapaxes(held[m, :, :, at : at + 128], 0, 1)

    owners = ye_ref.shape[0]
    each = slabs // owners
    zero = jnp.zeros((slabs, width), jnp.float32)
    rates = [ry_ref[m] for m in range(scales)]

    def widen(value):
        return jnp.concatenate([value] * (width // 128), axis=1)

    def step(y, state):
        fwd, bwd, power = state
        here = [w_ref[m, y] for m in range(scales)]
        fwd = tuple(widen(rates[m]) * fwd[m] + here[m] for m in range(scales))
        bwd = tuple(bwd[m] + widen(power[m]) * here[m] for m in range(scales))
        power = tuple(power[m] * rates[m] for m in range(scales))
        return fwd, bwd, power

    ones = jnp.ones((slabs, 128), jnp.float32)
    fwd, bwd, _ = lax.fori_loop(
        0, rows, step, ((zero,) * scales, (zero,) * scales, (ones,) * scales), unroll=4
    )
    for m in range(scales):
        for o in range(owners):
            mine = slice(o * each, (o + 1) * each)
            ye_ref[o, m * each : (m + 1) * each, :] = fwd[m][mine]
            ye_ref[o, (scales + m) * each : (scales + m + 1) * each, :] = bwd[m][mine]


def x_pass(ctrl, gathered, carry, inv_rows, rate_y, tile, width, subs):
    rows, slabs, cols = ctrl.shape
    scales = rate_y.shape[0]
    cols_n, _, edge_rows, _ = gathered.shape
    each = slabs // subs
    owners = group // each
    lanes = inv_rows.shape[2]
    return pl.pallas_call(
        functools.partial(x_kernel, tile, scales),
        grid=(slabs // group,),
        in_specs=[
            pl.BlockSpec((rows, group, cols), lambda i: (0, i, 0)),
            pl.BlockSpec((cols_n, group, edge_rows, rows), lambda i: (0, i, 0, 0)),
            pl.BlockSpec((group,) + carry.shape[1:], lambda i: (i, 0, 0)),
            pl.BlockSpec((group, 1, lanes), lambda i: (i, 0, 0)),
            pl.BlockSpec((scales, group, 128), lambda i: (0, i, 0)),
        ],
        out_specs=[
            pl.BlockSpec((scales, rows, group, width), lambda i: (0, 0, i, 0)),
            pl.BlockSpec((owners, 2 * scales * each, width), lambda i: (i, 0, 0)),
        ],
        out_shape=[
            jax.ShapeDtypeStruct((scales, rows, slabs, width), jnp.float32),
            jax.ShapeDtypeStruct((subs, 2 * scales * each, width), jnp.float32),
        ],
        scratch_shapes=[pltpu.VMEM((scales, group, rows, width), jnp.float32)],
        compiler_params=pltpu.CompilerParams(vmem_limit_bytes=vmem_bytes),
        name="x_pass",
    )(ctrl, gathered, carry, inv_rows, rate_y)


def greet(axis, size):
    me = lax.axis_index(axis)
    barrier = pltpu.get_barrier_semaphore()
    for k in range(1, size):
        pl.semaphore_signal(
            barrier, inc=1, device_id={axis: lax.rem(me + k, size)},
            device_id_type=pl.DeviceIdType.MESH,
        )
    pl.semaphore_wait(barrier, size - 1)


def send_all(axis, size, source, target, send_sems, recv_sems):
    me = lax.axis_index(axis)
    copies = []
    for k in range(1, size):
        partner = lax.rem(me + k, size)
        copies.append(
            pltpu.make_async_remote_copy(
                src_ref=source(partner), dst_ref=target.at[me],
                send_sem=send_sems.at[k], recv_sem=recv_sems.at[k],
                device_id={axis: partner}, device_id_type=pl.DeviceIdType.MESH,
            )
        )
        copies[-1].start()
    return copies


def gather_kernel(axis, size, own_ref, all_ref, send_sems, recv_sems):
    greet(axis, size)
    copies = send_all(axis, size, lambda p: own_ref, all_ref, send_sems, recv_sems)
    all_ref[lax.axis_index(axis)] = own_ref[...]
    for copy in copies:
        copy.wait()


def gather(own, axis):
    size = lax.axis_size(axis)
    vmem = pl.BlockSpec(memory_space=pltpu.VMEM)
    return pl.pallas_call(
        functools.partial(gather_kernel, axis, size),
        in_specs=[vmem],
        out_specs=vmem,
        out_shape=jax.ShapeDtypeStruct((size,) + own.shape, own.dtype),
        scratch_shapes=[pltpu.SemaphoreType.DMA((size,)), pltpu.SemaphoreType.DMA((size,))],
        compiler_params=pltpu.CompilerParams(
            collective_id=0, has_side_effects=True, vmem_limit_bytes=vmem_bytes
        ),
        name="x_gather",
    )(own)


def y_exchange_kernel(axis, size, edge_ref, rate_ref, out_ref, arrived, summed, *sems):
    me = lax.axis_index(axis)
    greet(axis, size)
    copies = send_all(axis, size, lambda p: edge_ref.at[p], arrived, sems[0], sems[1])
    arrived[me] = edge_ref[me]
    for copy in copies:
        copy.wait()
    half = edge_ref.shape[1] // 2
    width = edge_ref.shape[2]
    r, r_band, gain = [
        jnp.concatenate([rate_ref[k]] * (width // 128), axis=1) for k in range(3)
    ]
    value = jnp.zeros((half, width), jnp.float32)
    for a in range(size):
        summed[a, :half, :] = value
        value = r_band * value + arrived[a, :half, :]
    back = -r * value
    summed[size - 1, half:, :] = jnp.zeros((half, width), jnp.float32)
    for a in range(size - 1, 0, -1):
        back = r_band * back + arrived[a, half:, :]
        summed[a - 1, half:, :] = (r * summed[a, :half, :] + back) * gain
    copies = send_all(axis, size, lambda p: summed.at[p], out_ref, sems[2], sems[3])
    out_ref[me] = summed[me]
    for copy in copies:
        copy.wait()


def y_exchange(y_edges, inv, rows, axis):
    size = lax.axis_size(axis)
    r = jnp.exp(-inv)
    rates = jnp.stack([r, jnp.exp(-inv * rows), 1.0 / ((1.0 + r) * (1.0 - r))])
    rates = jnp.broadcast_to(rates[:, :, None], rates.shape + (128,))
    vmem = pl.BlockSpec(memory_space=pltpu.VMEM)
    shape = y_edges.shape
    return pl.pallas_call(
        functools.partial(y_exchange_kernel, axis, size),
        in_specs=[vmem] * 2,
        out_specs=vmem,
        out_shape=jax.ShapeDtypeStruct(shape, jnp.float32),
        scratch_shapes=[pltpu.VMEM(shape, jnp.float32)] * 2
        + [pltpu.SemaphoreType.DMA((size,))] * 4,
        compiler_params=pltpu.CompilerParams(
            collective_id=1, has_side_effects=True, vmem_limit_bytes=vmem_bytes
        ),
        name="y_exchange",
    )(y_edges, rates)


def y_kernel(scales, first_ref, w_ref, carry_ref, par_ref, inc_ref, wind_ref, held):
    _, rows, slabs, width = w_ref.shape
    cols = inc_ref.shape[2]

    def widen(value):
        return jnp.concatenate([value] * (width // 128), axis=1)

    rates = [par_ref[m] for m in range(scales)]
    gains = [par_ref[scales + m] for m in range(scales)]
    start = tuple(carry_ref[m] for m in range(scales))

    def ahead(y, state):
        state = tuple(widen(rates[m]) * state[m] + w_ref[m, y] for m in range(scales))
        for m in range(scales):
            held[m, y] = state[m]
        return state

    lax.fori_loop(0, rows, ahead, start, unroll=4)
    ends = tuple(carry_ref[scales + m] for m in range(scales))

    def mix(state):
        return sum(widen(gains[m]) * state[m] for m in range(scales))

    def back(i, state):
        y = rows - 1 - i
        state = tuple(widen(rates[m]) * state[m] + held[m, y] for m in range(scales))
        total = mix(state)
        here = total[:, :cols]
        inc_ref[y] = here
        east = pltpu.roll(total, width - 1, 1)[:, :cols] - pltpu.roll(total, 1, 1)[:, :cols]
        wind_ref[1, y] = (2.0 * east).astype(jnp.bfloat16)
        return state

    state = lax.fori_loop(0, rows, back, ends, unroll=4)
    below = mix(ends)[:, :cols]
    above = mix(tuple(widen(rates[m]) * state[m] + start[m] for m in range(scales)))[:, :cols]
    above = jnp.where(first_ref[0] == 1, 0.0, above)
    wind_ref[0, 0] = (-2.0 * (inc_ref[1] - above)).astype(jnp.bfloat16)
    wind_ref[0, rows - 1] = (-2.0 * (below - inc_ref[rows - 2])).astype(jnp.bfloat16)

    def north(y, _):
        wind_ref[0, y] = (-2.0 * (inc_ref[y + 1] - inc_ref[y - 1])).astype(jnp.bfloat16)
        return _

    lax.fori_loop(1, rows - 1, north, 0, unroll=2)


def y_pass(first, smoothed, carries, params, cols):
    scales, rows, slabs, width = smoothed.shape
    block = 16
    return pl.pallas_call(
        functools.partial(y_kernel, scales),
        grid=(slabs // block,),
        in_specs=[
            pl.BlockSpec(memory_space=pltpu.SMEM),
            pl.BlockSpec((scales, rows, block, width), lambda i: (0, 0, i, 0)),
            pl.BlockSpec((2 * scales, block, width), lambda i: (0, i, 0)),
            pl.BlockSpec((2 * scales, block, 128), lambda i: (0, i, 0)),
        ],
        out_specs=[
            pl.BlockSpec((rows, block, cols), lambda i: (0, i, 0)),
            pl.BlockSpec((2, rows, block, cols), lambda i: (0, 0, i, 0)),
        ],
        out_shape=[
            jax.ShapeDtypeStruct((rows, slabs, cols), jnp.float32),
            jax.ShapeDtypeStruct((2, rows, slabs, cols), jnp.bfloat16),
        ],
        scratch_shapes=[pltpu.VMEM((scales, rows, block, width), jnp.float32)],
        compiler_params=pltpu.CompilerParams(vmem_limit_bytes=vmem_bytes),
        name="y_pass",
    )(first, smoothed, carries, params)


def per_device(control, scale_index, length_x, length_y, scale_weight):
    inv_x, inv_y, amplitude = slab_coefficients(scale_index, length_x, length_y, scale_weight)
    subs, cols_n = lax.axis_size("sub"), lax.axis_size("col")
    rows, cols, slabs = control.shape
    scales = inv_x.shape[1]
    tile = 128 if cols % 128 == 0 else cols
    local = cols // tile
    width = (cols // 128 + 1) * 128
    each = slabs // subs
    me = lax.axis_index("sub")
    ctrl = control.transpose(0, 2, 1)
    edges = x_edges(ctrl, edge_weights(inv_x, tile).transpose(0, 2, 1), tile)
    gathered = gather(edges, "col")
    carry = carry_matrix(inv_x, tile, local, cols_n, lax.axis_index("col"))
    inv_rows = jnp.repeat(inv_x, tile, axis=1)[:, None, :]
    rate = jnp.exp(-inv_y)
    rate_y = jnp.broadcast_to(rate.T[:, :, None], (scales, slabs, 128))
    smoothed, y_edges = x_pass(ctrl, gathered, carry, inv_rows, rate_y, tile, width, subs)
    owned = lax.dynamic_slice_in_dim(inv_y, me * each, each, 0).T.reshape(scales * each)
    returned = y_exchange(y_edges, owned, rows, "sub")
    carries = returned.reshape(subs, 2 * scales, each, width).transpose(1, 0, 2, 3)
    carries = carries.reshape(2 * scales, slabs, width)
    gain = (amplitude * (1.0 - rate) * (1.0 - rate)).T
    gain = jnp.broadcast_to(gain[:, :, None], (scales, slabs, 128))
    params = jnp.concatenate([rate_y, gain], axis=0)
    first = (me == 0).astype(jnp.int32)[None]
    increment, wind = y_pass(first, smoothed, carries, params, cols)
    return (increment.transpose(0, 2, 1), wind.transpose(0, 1, 3, 2))


def solution(mesh):
    placed = (P("sub", "col", None), P(), P(), P(), P())
    return jax.shard_map(
        per_device,
        mesh=mesh,
        in_specs=placed,
        out_specs=(P("sub", "col", None), P(None, "sub", "col", None)),
        check_vma=False,
    )
```
